32 devices in a mesh: clip: 2 (over x), frame: 16 (over z, y, core).
Axes of the slice: x: 2, y: 2, z: 4, core: 2. Of those that a mesh axis runs over, the one named last changes fastest.
Arguments:
- queries: bfloat16 [16384, 2560], P(('clip', 'frame')), parts along dimension 0, may hold values from -12 to 12
- key_rows: bfloat16 [16384, 2560], P(('clip', 'frame')), parts along dimension 0, may hold values from -12 to 12
- values: bfloat16 [16384, 2560], P(('clip', 'frame')), parts along dimension 0, may hold values from -6 to 6
- block_lists: int32 [128, 8], P(('clip', 'frame')), parts along dimension 0, may hold values from -1 to 63, as said below
Outputs:
- attended: bfloat16 [16384, 2560], P(('clip', 'frame')), parts along dimension 0
The draws below stay inside these ranges and needn't reach their ends.
There are 2 independent parts, one for each index of `clip`. The reference program is written for one: setup_inputs(seed, part) draws one part's arguments, and reference() takes and returns one part's arrays. A program takes and returns all parts, laid end to end along the dimension named above; each array names one. Nothing has to cross between parts.
Inputs may be any that keep to these rules, and one draw needn't show every extreme that they name: `block_lists`: each row names distinct blocks in no particular order, -1 marking an empty slot. Row r names every block of its own device j = r // 4 (blocks 4 * j to 4 * j + 3) and otherwise only blocks of devices at most 2 away. Over the 4 rows of one device, the blocks named that lie on any one other device number at most 1.
All inputs are finite; a program needn't handle non-finite values.
Results may differ from the reference program's by a relative error of at most 0.0046.
Values may be sent and summed in bfloat16 or wider, within the bound.
A program may use at most 128 MiB of HBM per device.

```python
import jax
import jax.numpy as jnp
from jax import lax

HEADS = 20
HD = 128
BLK = 128
QB_DEV = 4
REACH = 2
CAP = 1
KPB = 8
W = 2560
TOKENS = 8192
NBLK = 64


def draw_queries(key, part):
    key = jax.random.fold_in(key, 1)
    return jnp.clip(jax.random.normal(key, (TOKENS, HEADS * HD), jnp.float32), -6.0, 6.0).astype(jnp.bfloat16)


def draw_key_rows(key, part):
    key = jax.random.fold_in(key, 2)
    return jnp.clip(jax.random.normal(key, (TOKENS, HEADS * HD), jnp.float32), -6.0, 6.0).astype(jnp.bfloat16)


def draw_block_lists(key, part):
    key = jax.random.fold_in(key, 11)
    key_one, key_two, key_three = jax.random.split(key, 3)
    device_count = NBLK // QB_DEV
    offset_list = []
    for distance in range(1, REACH + 1):
        offset_list.append(-distance)
        offset_list.append(distance)
    offset_values = jnp.array(offset_list, dtype=jnp.int32)
    offset_count = len(offset_list)
    ranking = jax.random.randint(key_one, (device_count, offset_count, QB_DEV), 0, 1 << 20) * QB_DEV + jnp.arange(QB_DEV)
    ordering = jnp.argsort(ranking, axis=-1, stable=True)
    chosen = ordering[:, :, :CAP]
    device_ids = jnp.arange(device_count)
    target = device_ids[:, None] + offset_values[None, :]
    inside = (target >= 0) & (target < device_count)
    far_blocks = target[:, :, None] * QB_DEV + chosen
    query_ids = jnp.arange(NBLK)
    query_device = query_ids // QB_DEV
    query_local = query_ids % QB_DEV
    distance_values = jnp.abs(offset_values)
    coin_draws = jax.random.randint(key_two, (NBLK, offset_count, CAP), 0, REACH + 1)
    kept = coin_draws < (REACH + 1 - distance_values)[None, :, None]
    forced = (query_local == 0)[:, None, None] & (distance_values == 1)[None, :, None]
    kept = (kept | forced) & inside[query_device][:, :, None]
    far_entries = jnp.where(kept, far_blocks[query_device], -1).reshape(NBLK, offset_count * CAP)
    own_entries = query_device[:, None] * QB_DEV + jnp.arange(QB_DEV)[None, :]
    entries = jnp.concatenate([own_entries, far_entries], axis=1)
    shuffle_scores = jax.random.randint(key_three, (NBLK, KPB), 0, 1 << 20) * KPB + jnp.arange(KPB)[None, :]
    shuffle = jnp.argsort(shuffle_scores, axis=1, stable=True)
    return jnp.take_along_axis(entries, shuffle, axis=1).astype(jnp.int32)


def block_levels(stream_key, shape, cuts, least, high):
    gain, own = 1.0, jax.random.fold_in(stream_key, 6)
    for dim, blocks in cuts:
        heights = jnp.exp(jax.random.uniform(jax.random.fold_in(own, dim), (blocks,), jnp.float32, least / len(cuts), high / len(cuts)))
        gain = gain * jnp.repeat(heights, shape[dim] // blocks).reshape([-1 if axis == dim else 1 for axis in range(len(shape))])
    return gain


def centred(key, extent, spread, most, cuts=(), kind=jnp.bfloat16):
    values = spread * jax.random.normal(key, extent, jnp.float32)
    if cuts:
        values = values * block_levels(key, extent, cuts, -0.22, 0.18)
    return jnp.clip(values, -most, most).astype(kind)


def setup_inputs(seed: int = 0, part: int = 0) -> dict:
    key_list = jax.random.split(jax.random.key(seed), 5)
    part_splits = jax.random.split(jax.random.fold_in(key_list[4], part), 5)
    return {
        "queries": draw_queries(jax.random.fold_in(jax.random.fold_in(key_list[4], part), 71), part),
        "key_rows": draw_key_rows(jax.random.fold_in(jax.random.fold_in(key_list[4], part), 71), part),
        "values": centred(part_splits[2], (TOKENS, W), 1.0, 6.0, ((0, 16),)),
        "block_lists": draw_block_lists(jax.random.fold_in(jax.random.fold_in(key_list[4], part), 71), part),
    }


def reference(queries, key_rows, values, block_lists):
    head_count = queries.shape[1] // HD
    query_blocks = queries.reshape(NBLK, BLK, head_count, HD)
    key_blocks = key_rows.reshape(NBLK, BLK, head_count, HD)
    value_blocks = values.reshape(NBLK, BLK, head_count, HD)
    score_scale = HD ** -0.5

    def one_block(inputs):
        query_part, named = inputs
        safe_ids = jnp.maximum(named, 0).astype(jnp.int32)
        gathered_keys = key_blocks[safe_ids].reshape(KPB * BLK, head_count, HD).astype(jnp.float32)
        gathered_values = value_blocks[safe_ids].reshape(KPB * BLK, head_count, HD).astype(jnp.float32)
        allowed = jnp.broadcast_to((named >= 0)[:, None], (KPB, BLK)).reshape(KPB * BLK)
        scores = jnp.einsum("qhd,khd->hqk", query_part.astype(jnp.float32), gathered_keys,
                            precision=lax.Precision.HIGHEST) * score_scale
        scores = jnp.where(allowed[None, None, :], scores, -jnp.inf)
        row_peak = jnp.max(scores, axis=2, keepdims=True)
        weights = jnp.where(allowed[None, None, :], jnp.exp(scores - row_peak), 0.0)
        row_total = jnp.sum(weights, axis=2, keepdims=True)
        rounded = lax.optimization_barrier(weights.astype(jnp.bfloat16)).astype(jnp.float32)
        attended = jnp.einsum("hqk,khd->qhd", rounded, gathered_values, precision=lax.Precision.HIGHEST)
        attended = attended / jnp.transpose(row_total, (1, 0, 2))
        return attended.reshape(BLK, head_count * HD).astype(jnp.bfloat16)

    result = lax.map(one_block, (query_blocks, block_lists))
    return result.reshape(NBLK * BLK, head_count * HD)
```

```python
import functools
import math

import jax
import jax.numpy as jnp
from jax import lax
from jax.experimental import pallas as pl
from jax.experimental.pallas import tpu as pltpu
from jax.sharding import PartitionSpec as P

HD = 128
REACH = 2
GROUP_HEADS = 2
OFFSETS = (-1, 1, -2, 2)
SLOTS = len(OFFSETS)


def kernel(
    size,
    q_hbm,
    k_hbm,
    v_hbm,
    lists_smem,
    lists_vmem,
    out_hbm,
    q_ref,
    k_ref,
    v_ref,
    out_ref,
    named_vmem,
    named_smem,
    send_ref,
    recv_ref,
    acc_ref,
    peak_ref,
    total_ref,
    bias_ref,
    pick_ref,
    load_sem,
    list_send_sem,
    list_recv_sem,
    smem_sem,
    send_sem,
    recv_sem,
    out_sem,
):
    me = lax.axis_index("frame")
    per_device, slots_row = lists_smem.shape
    tokens = q_ref.shape[0]
    block = tokens // per_device
    groups = recv_ref.shape[0]
    group_width = recv_ref.shape[3]
    scale = HD ** (-0.5) * math.log2(math.e)

    def inside(slot):
        other = me + OFFSETS[slot]
        return (other >= 0) & (other < size)

    loads = [
        pltpu.make_async_copy(k_hbm, k_ref, load_sem.at[0]),
        pltpu.make_async_copy(v_hbm, v_ref, load_sem.at[1]),
        pltpu.make_async_copy(q_hbm, q_ref, load_sem.at[2]),
    ]
    for load in loads:
        load.start()

    barrier = pltpu.get_barrier_semaphore()
    count = jnp.int32(0)
    for slot in range(SLOTS):
        present = inside(slot)
        count = count + present.astype(jnp.int32)

        @pl.when(present)
        def _():
            pl.semaphore_signal(
                barrier,
                inc=1,
                device_id={"frame": me + OFFSETS[slot]},
                device_id_type=pl.DeviceIdType.MESH,
            )

    pl.semaphore_wait(barrier, count)

    def list_copy(slot):
        return pltpu.make_async_remote_copy(
            src_ref=lists_vmem,
            dst_ref=named_vmem.at[slot ^ 1],
            send_sem=list_send_sem.at[slot],
            recv_sem=list_recv_sem.at[slot ^ 1],
            device_id={"frame": me + OFFSETS[slot]},
            device_id_type=pl.DeviceIdType.MESH,
        )

    def list_arrival(slot):
        return pltpu.make_async_remote_copy(
            src_ref=lists_vmem,
            dst_ref=named_vmem.at[slot],
            send_sem=list_send_sem.at[slot],
            recv_sem=list_recv_sem.at[slot],
            device_id={"frame": me + OFFSETS[slot]},
            device_id_type=pl.DeviceIdType.MESH,
        )

    for slot in range(SLOTS):

        @pl.when(inside(slot))
        def _():
            list_copy(slot).start()

        @pl.when(jnp.logical_not(inside(slot)))
        def _():
            named_vmem[slot] = jnp.full((per_device, slots_row), -1, jnp.int32)
            for part in range(2):
                recv_ref[:, part, slot * block : (slot + 1) * block, :] = jnp.zeros(
                    (groups, block, group_width), jnp.bfloat16
                )

    for row in range(per_device):
        entries = [lists_smem[row, column] for column in range(slots_row)]
        for slot in range(SLOTS):
            first = (me + OFFSETS[slot]) * per_device
            named = jnp.bool_(False)
            for entry in entries:
                named = named | ((entry >= 0) & (entry >= first) & (entry < first + per_device))
            bias_ref[row * block : (row + 1) * block, slot * block : (slot + 1) * block] = jnp.full(
                (block, block), jnp.where(named, 0.0, -jnp.inf), jnp.float32
            )

    for slot in range(SLOTS):

        @pl.when(inside(slot))
        def _():
            list_arrival(slot).wait_recv()

    to_smem = pltpu.make_async_copy(named_vmem, named_smem, smem_sem)
    to_smem.start()
    to_smem.wait()

    for slot in range(SLOTS):
        chosen = jnp.int32(0)
        for row in range(per_device):
            for column in range(slots_row):
                local_id = named_smem[slot, row, column] - me * per_device
                chosen = jnp.where((local_id >= 0) & (local_id < per_device), local_id, chosen)
        for place in range(per_device):
            pick_ref[slot, place] = jnp.full(
                (block, group_width), jnp.where(chosen == place, 1.0, 0.0), jnp.float32
            ).astype(jnp.bfloat16)

    loads[0].wait()
    loads[1].wait()

    def block_copy(group, slot):
        return pltpu.make_async_remote_copy(
            src_ref=send_ref.at[slot, group],
            dst_ref=recv_ref.at[group, :, pl.ds((slot ^ 1) * block, block), :],
            send_sem=send_sem.at[slot, group],
            recv_sem=recv_sem.at[slot ^ 1, group],
            device_id={"frame": me + OFFSETS[slot]},
            device_id_type=pl.DeviceIdType.MESH,
        )

    def block_arrival(group, slot):
        return pltpu.make_async_remote_copy(
            src_ref=send_ref.at[slot, group],
            dst_ref=recv_ref.at[group, :, pl.ds(slot * block, block), :],
            send_sem=send_sem.at[slot, group],
            recv_sem=recv_sem.at[slot, group],
            device_id={"frame": me + OFFSETS[slot]},
            device_id_type=pl.DeviceIdType.MESH,
        )

    def send_group(group, carry):
        columns = pl.ds(pl.multiple_of(group * group_width, group_width), group_width)
        for slot in (2, 3, 0, 1):

            @pl.when(inside(slot))
            def _():
                for part, source in enumerate((k_ref, v_ref)):
                    picked = source[0:block, columns] * pick_ref[slot, 0]
                    for place in range(1, per_device):
                        rows = slice(place * block, (place + 1) * block)
                        picked = picked + source[rows, columns] * pick_ref[slot, place]
                    send_ref[slot, group, part] = picked
                block_copy(group, slot).start()

        return carry

    lax.fori_loop(0, groups, send_group, 0)

    loads[2].wait()

    def own_head(head, carry):
        columns = pl.ds(pl.multiple_of(head * HD, HD), HD)
        scores = lax.dot_general(
            q_ref[:, columns],
            k_ref[:, columns],
            (((1,), (1,)), ((), ())),
            preferred_element_type=jnp.float32,
        )
        peak = jnp.max(scores, axis=1, keepdims=True)
        weights = jnp.exp2((scores - peak) * scale)
        peak_ref[head] = peak
        total_ref[head] = jnp.sum(weights, axis=1, keepdims=True)
        acc_ref[:, columns] = jnp.dot(
            weights.astype(jnp.bfloat16), v_ref[:, columns], preferred_element_type=jnp.float32
        )
        return carry

    lax.fori_loop(0, groups * GROUP_HEADS, own_head, 0)

    def out_copy(group):
        columns = pl.ds(pl.multiple_of(group * group_width, group_width), group_width)
        return pltpu.make_async_copy(
            out_ref.at[:, columns], out_hbm.at[:, columns], out_sem.at[group]
        )

    def far_group(group, carry):
        for slot in range(SLOTS):

            @pl.when(inside(slot))
            def _():
                block_arrival(group, slot).wait_recv()

        for step in range(GROUP_HEADS):
            head = group * GROUP_HEADS + step
            columns = pl.ds(pl.multiple_of(head * HD, HD), HD)
            far_columns = slice(step * HD, (step + 1) * HD)
            scores = lax.dot_general(
                q_ref[:, columns],
                recv_ref[group, 0, :, far_columns],
                (((1,), (1,)), ((), ())),
                preferred_element_type=jnp.float32,
            )
            scores = scores + bias_ref[...]
            own_peak = peak_ref[head]
            peak = jnp.maximum(jnp.max(scores, axis=1, keepdims=True), own_peak)
            weights = jnp.exp2((scores - peak) * scale)
            shrink = jnp.exp2((own_peak - peak) * scale)
            total = total_ref[head] * shrink + jnp.sum(weights, axis=1, keepdims=True)
            far = jnp.dot(
                weights.astype(jnp.bfloat16),
                recv_ref[group, 1, :, far_columns],
                preferred_element_type=jnp.float32,
            )
            attended = (acc_ref[:, columns] * shrink + far) / total
            out_ref[:, columns] = attended.astype(jnp.bfloat16)
        out_copy(group).start()
        return carry

    lax.fori_loop(0, groups, far_group, 0)

    def finish(group, carry):
        for slot in range(SLOTS):

            @pl.when(inside(slot))
            def _():
                block_copy(group, slot).wait_send()

        out_copy(group).wait()
        return carry

    lax.fori_loop(0, groups, finish, 0)
    for slot in range(SLOTS):

        @pl.when(inside(slot))
        def _():
            list_copy(slot).wait_send()


def local(size, queries, key_rows, values, block_lists):
    tokens, width = queries.shape
    per_device, slots_row = block_lists.shape
    block = tokens // per_device
    heads = width // HD
    groups = heads // GROUP_HEADS
    group_width = GROUP_HEADS * HD
    far = SLOTS * block
    hbm = pl.BlockSpec(memory_space=pl.ANY)
    return pl.pallas_call(
        functools.partial(kernel, size),
        out_shape=jax.ShapeDtypeStruct((tokens, width), jnp.bfloat16),
        in_specs=[
            hbm,
            hbm,
            hbm,
            pl.BlockSpec(memory_space=pltpu.SMEM),
            pl.BlockSpec(memory_space=pltpu.VMEM),
        ],
        out_specs=hbm,
        scratch_shapes=[
            pltpu.VMEM((tokens, width), jnp.bfloat16),
            pltpu.VMEM((tokens, width), jnp.bfloat16),
            pltpu.VMEM((tokens, width), jnp.bfloat16),
            pltpu.VMEM((tokens, width), jnp.bfloat16),
            pltpu.VMEM((SLOTS, per_device, slots_row), jnp.int32),
            pltpu.SMEM((SLOTS, per_device, slots_row), jnp.int32),
            pltpu.VMEM((SLOTS, groups, 2, block, group_width), jnp.bfloat16),
            pltpu.VMEM((groups, 2, far, group_width), jnp.bfloat16),
            pltpu.VMEM((tokens, width), jnp.float32),
            pltpu.VMEM((heads, tokens, 1), jnp.float32),
            pltpu.VMEM((heads, tokens, 1), jnp.float32),
            pltpu.VMEM((tokens, far), jnp.float32),
            pltpu.VMEM((SLOTS, per_device, block, group_width), jnp.bfloat16),
            pltpu.SemaphoreType.DMA((3,)),
            pltpu.SemaphoreType.DMA((SLOTS,)),
            pltpu.SemaphoreType.DMA((SLOTS,)),
            pltpu.SemaphoreType.DMA,
            pltpu.SemaphoreType.DMA((SLOTS, groups)),
            pltpu.SemaphoreType.DMA((SLOTS, groups)),
            pltpu.SemaphoreType.DMA((groups,)),
        ],
        compiler_params=pltpu.CompilerParams(
            collective_id=0, has_side_effects=True, vmem_limit_bytes=56 * 1024 * 1024
        ),
        cost_estimate=pl.CostEstimate(
            flops=4 * tokens * (tokens + far) * width,
            bytes_accessed=4 * tokens * width * 2,
            transcendentals=heads * tokens * (tokens + far),
        ),
    )(queries, key_rows, values, block_lists, block_lists)


def solution(mesh):
    rows = P(("clip", "frame"), None)
    return jax.shard_map(
        functools.partial(local, mesh.shape["frame"]),
        mesh=mesh,
        in_specs=(rows, rows, rows, rows),
        out_specs=rows,
        check_vma=False,
    )
```

```python
import functools
import math

import jax
import jax.numpy as jnp
from jax import lax
from jax.experimental import pallas as pl
from jax.experimental.pallas import tpu as pltpu
from jax.sharding import PartitionSpec as P

HD = 128
REACH = 2
QUAD = 4
MOST_QUADS = 4
GROUP_HEADS = 1
OFFSETS = (-1, 1, -2, 2)
SLOTS = len(OFFSETS)


def kernel(
    size,
    q_hbm,
    k_hbm,
    v_hbm,
    lists_smem,
    lists_vmem,
    out_hbm,
    q_ref,
    k_ref,
    v_ref,
    out_ref,
    named_vmem,
    named_smem,
    send_ref,
    recv_ref,
    acc_ref,
    peak_ref,
    total_ref,
    bias_ref,
    pick_ref,
    relay_ref,
    load_sem,
    list_send_sem,
    list_recv_sem,
    smem_sem,
    send_sem,
    recv_sem,
    relay_recv_sem,
    forward_sem,
    out_sem,
):
    me = lax.axis_index("frame")
    per_device, slots_row = lists_smem.shape
    tokens = q_ref.shape[0]
    block = tokens // per_device
    groups = recv_ref.shape[0]
    group_width = recv_ref.shape[3]
    scale = HD ** (-0.5) * math.log2(math.e)

    def inside(slot):
        other = me + OFFSETS[slot]
        return (other >= 0) & (other < size)

    loads = [
        pltpu.make_async_copy(k_hbm, k_ref, load_sem.at[0]),
        pltpu.make_async_copy(v_hbm, v_ref, load_sem.at[1]),
        pltpu.make_async_copy(q_hbm, q_ref, load_sem.at[2]),
    ]
    for load in loads:
        load.start()

    quads = size // QUAD
    quad = me // QUAD
    relays = size % QUAD == 0 and quads <= MOST_QUADS

    def by_relay(group, upward):
        share = jnp.where(upward, quads - 1 - quad, quad)
        back = groups - 1 - group
        return (back + 1) * share // quads > back * share // quads

    def relayed(group, slot):
        other = me + OFFSETS[slot]
        return (other // QUAD != quad) & by_relay(group, OFFSETS[slot] > 0)

    lower = me % QUAD < QUAD // 2
    sign = jnp.where(lower, 1, -1)

    def forward_target(flow):
        return me + sign * (QUAD // 2 + 1 + flow)

    def forwards(group, flow):
        target = forward_target(flow)
        return (
            (target >= 0)
            & (target < size)
            & (target // QUAD == quad + sign)
            & by_relay(group, lower)
        )

    barrier = pltpu.get_barrier_semaphore()
    count = jnp.int32(0)
    span = REACH + QUAD // 2 if relays else REACH
    for offset in [o for o in range(-span, span + 1) if o]:
        present = (me + offset >= 0) & (me + offset < size)
        count = count + present.astype(jnp.int32)

        @pl.when(present)
        def _():
            pl.semaphore_signal(
                barrier,
                inc=1,
                device_id={"frame": me + offset},
                device_id_type=pl.DeviceIdType.MESH,
            )

    pl.semaphore_wait(barrier, count)

    def list_copy(slot):
        return pltpu.make_async_remote_copy(
            src_ref=lists_vmem,
            dst_ref=named_vmem.at[slot ^ 1],
            send_sem=list_send_sem.at[slot],
            recv_sem=list_recv_sem.at[slot ^ 1],
            device_id={"frame": me + OFFSETS[slot]},
            device_id_type=pl.DeviceIdType.MESH,
        )

    def list_arrival(slot):
        return pltpu.make_async_remote_copy(
            src_ref=lists_vmem,
            dst_ref=named_vmem.at[slot],
            send_sem=list_send_sem.at[slot],
            recv_sem=list_recv_sem.at[slot],
            device_id={"frame": me + OFFSETS[slot]},
            device_id_type=pl.DeviceIdType.MESH,
        )

    for slot in range(SLOTS):

        @pl.when(inside(slot))
        def _():
            list_copy(slot).start()

        @pl.when(jnp.logical_not(inside(slot)))
        def _():
            named_vmem[slot] = jnp.full((per_device, slots_row), -1, jnp.int32)
            for part in range(2):
                recv_ref[:, part, slot * block : (slot + 1) * block, :] = jnp.zeros(
                    (groups, block, group_width), jnp.bfloat16
                )

    for row in range(per_device):
        entries = [lists_smem[row, column] for column in range(slots_row)]
        for slot in range(SLOTS):
            first = (me + OFFSETS[slot]) * per_device
            named = jnp.bool_(False)
            for entry in entries:
                named = named | ((entry >= 0) & (entry >= first) & (entry < first + per_device))
            bias_ref[row * block : (row + 1) * block, slot * block : (slot + 1) * block] = jnp.full(
                (block, block), jnp.where(named, 0.0, -jnp.inf), jnp.float32
            )

    for slot in range(SLOTS):

        @pl.when(inside(slot))
        def _():
            list_arrival(slot).wait_recv()

    to_smem = pltpu.make_async_copy(named_vmem, named_smem, smem_sem)
    to_smem.start()
    to_smem.wait()

    for slot in range(SLOTS):
        chosen = jnp.int32(0)
        for row in range(per_device):
            for column in range(slots_row):
                local_id = named_smem[slot, row, column] - me * per_device
                chosen = jnp.where((local_id >= 0) & (local_id < per_device), local_id, chosen)
        for place in range(per_device):
            pick_ref[slot, place] = jnp.full(
                (block, group_width), jnp.where(chosen == place, 1.0, 0.0), jnp.float32
            ).astype(jnp.bfloat16)

    loads[0].wait()
    loads[1].wait()

    def block_copy(group, slot):
        return pltpu.make_async_remote_copy(
            src_ref=send_ref.at[slot, group],
            dst_ref=recv_ref.at[group, :, pl.ds((slot ^ 1) * block, block), :],
            send_sem=send_sem.at[slot, group],
            recv_sem=recv_sem.at[slot ^ 1, group],
            device_id={"frame": me + OFFSETS[slot]},
            device_id_type=pl.DeviceIdType.MESH,
        )

    def block_arrival(group, slot):
        return pltpu.make_async_remote_copy(
            src_ref=send_ref.at[slot, group],
            dst_ref=recv_ref.at[group, :, pl.ds(slot * block, block), :],
            send_sem=send_sem.at[slot, group],
            recv_sem=recv_sem.at[slot, group],
            device_id={"frame": me + OFFSETS[slot]},
            device_id_type=pl.DeviceIdType.MESH,
        )

    def relay_copy(group, slot):
        step = QUAD // 2 if OFFSETS[slot] < 0 else -(QUAD // 2)
        flow = abs(OFFSETS[slot]) - 1
        return pltpu.make_async_remote_copy(
            src_ref=send_ref.at[slot, group],
            dst_ref=relay_ref.at[flow, group],
            send_sem=send_sem.at[slot, group],
            recv_sem=relay_recv_sem.at[flow, group],
            device_id={"frame": me + step},
            device_id_type=pl.DeviceIdType.MESH,
        )

    def relay_arrival(group, flow):
        return pltpu.make_async_remote_copy(
            src_ref=relay_ref.at[flow, group],
            dst_ref=relay_ref.at[flow, group],
            send_sem=forward_sem.at[flow, group],
            recv_sem=relay_recv_sem.at[flow, group],
            device_id={"frame": forward_target(flow)},
            device_id_type=pl.DeviceIdType.MESH,
        )

    def forward_copy(group, flow):
        slot = 2 * flow + jnp.where(lower, 0, 1)
        return pltpu.make_async_remote_copy(
            src_ref=relay_ref.at[flow, group],
            dst_ref=recv_ref.at[group, :, pl.ds(pl.multiple_of(slot * block, block), block), :],
            send_sem=forward_sem.at[flow, group],
            recv_sem=recv_sem.at[slot, group],
            device_id={"frame": forward_target(flow)},
            device_id_type=pl.DeviceIdType.MESH,
        )

    def forward_group(group):
        for flow in range(REACH):

            @pl.when(forwards(group, flow))
            def _():
                relay_arrival(group, flow).wait_recv()
                forward_copy(group, flow).start()

    def send_group(group, carry):
        columns = pl.ds(pl.multiple_of(group * group_width, group_width), group_width)
        for slot in (2, 3, 0, 1):

            @pl.when(inside(slot))
            def _():
                for part, source in enumerate((k_ref, v_ref)):
                    picked = source[0:block, columns] * pick_ref[slot, 0]
                    for place in range(1, per_device):
                        rows = slice(place * block, (place + 1) * block)
                        picked = picked + source[rows, columns] * pick_ref[slot, place]
                    send_ref[slot, group, part] = picked
                if relays:
                    far_way = relayed(group, slot)

                    @pl.when(far_way)
                    def _():
                        relay_copy(group, slot).start()

                    @pl.when(jnp.logical_not(far_way))
                    def _():
                        block_copy(group, slot).start()

                else:
                    block_copy(group, slot).start()

        return carry

    lax.fori_loop(0, groups, send_group, 0)

    loads[2].wait()

    def own_head(head, carry):
        columns = pl.ds(pl.multiple_of(head * HD, HD), HD)
        scores = lax.dot_general(
            q_ref[:, columns],
            k_ref[:, columns],
            (((1,), (1,)), ((), ())),
            preferred_element_type=jnp.float32,
        )
        peak = jnp.max(scores, axis=1, keepdims=True)
        weights = jnp.exp2((scores - peak) * scale)
        peak_ref[head] = peak
        total_ref[head] = jnp.sum(weights, axis=1, keepdims=True)
        acc_ref[:, columns] = jnp.dot(
            weights.astype(jnp.bfloat16), v_ref[:, columns], preferred_element_type=jnp.float32
        )
        return carry

    lax.fori_loop(0, groups * GROUP_HEADS, own_head, 0)

    def out_copy(group):
        columns = pl.ds(pl.multiple_of(group * group_width, group_width), group_width)
        return pltpu.make_async_copy(
            out_ref.at[:, columns], out_hbm.at[:, columns], out_sem.at[group]
        )

    def far_group(group, carry):
        if relays:
            forward_group(group)
        for slot in range(SLOTS):

            @pl.when(inside(slot))
            def _():
                block_arrival(group, slot).wait_recv()

        for step in range(GROUP_HEADS):
            head = group * GROUP_HEADS + step
            columns = pl.ds(pl.multiple_of(head * HD, HD), HD)
            far_columns = slice(step * HD, (step + 1) * HD)
            scores = lax.dot_general(
                q_ref[:, columns],
                recv_ref[group, 0, :, far_columns],
                (((1,), (1,)), ((), ())),
                preferred_element_type=jnp.float32,
            )
            scores = scores + bias_ref[...]
            own_peak = peak_ref[head]
            peak = jnp.maximum(jnp.max(scores, axis=1, keepdims=True), own_peak)
            weights = jnp.exp2((scores - peak) * scale)
            shrink = jnp.exp2((own_peak - peak) * scale)
            total = total_ref[head] * shrink + jnp.sum(weights, axis=1, keepdims=True)
            far = jnp.dot(
                weights.astype(jnp.bfloat16),
                recv_ref[group, 1, :, far_columns],
                preferred_element_type=jnp.float32,
            )
            attended = (acc_ref[:, columns] * shrink + far) / total
            out_ref[:, columns] = attended.astype(jnp.bfloat16)
        out_copy(group).start()
        return carry

    lax.fori_loop(0, groups, far_group, 0)

    def finish(group, carry):
        for slot in range(SLOTS):

            @pl.when(inside(slot))
            def _():
                block_copy(group, slot).wait_send()

        if relays:
            for flow in range(REACH):

                @pl.when(forwards(group, flow))
                def _():
                    forward_copy(group, flow).wait_send()

        out_copy(group).wait()
        return carry

    lax.fori_loop(0, groups, finish, 0)
    for slot in range(SLOTS):

        @pl.when(inside(slot))
        def _():
            list_copy(slot).wait_send()


def local(size, queries, key_rows, values, block_lists):
    tokens, width = queries.shape
    per_device, slots_row = block_lists.shape
    block = tokens // per_device
    heads = width // HD
    groups = heads // GROUP_HEADS
    group_width = GROUP_HEADS * HD
    far = SLOTS * block
    hbm = pl.BlockSpec(memory_space=pl.ANY)
    return pl.pallas_call(
        functools.partial(kernel, size),
        out_shape=jax.ShapeDtypeStruct((tokens, width), jnp.bfloat16),
        in_specs=[
            hbm,
            hbm,
            hbm,
            pl.BlockSpec(memory_space=pltpu.SMEM),
            pl.BlockSpec(memory_space=pltpu.VMEM),
        ],
        out_specs=hbm,
        scratch_shapes=[
            pltpu.VMEM((tokens, width), jnp.bfloat16),
            pltpu.VMEM((tokens, width), jnp.bfloat16),
            pltpu.VMEM((tokens, width), jnp.bfloat16),
            pltpu.VMEM((tokens, width), jnp.bfloat16),
            pltpu.VMEM((SLOTS, per_device, slots_row), jnp.int32),
            pltpu.SMEM((SLOTS, per_device, slots_row), jnp.int32),
            pltpu.VMEM((SLOTS, groups, 2, block, group_width), jnp.bfloat16),
            pltpu.VMEM((groups, 2, far, group_width), jnp.bfloat16),
            pltpu.VMEM((tokens, width), jnp.float32),
            pltpu.VMEM((heads, tokens, 1), jnp.float32),
            pltpu.VMEM((heads, tokens, 1), jnp.float32),
            pltpu.VMEM((tokens, far), jnp.float32),
            pltpu.VMEM((SLOTS, per_device, block, group_width), jnp.bfloat16),
            pltpu.VMEM((REACH, groups, 2, block, group_width), jnp.bfloat16),
            pltpu.SemaphoreType.DMA((3,)),
            pltpu.SemaphoreType.DMA((SLOTS,)),
            pltpu.SemaphoreType.DMA((SLOTS,)),
            pltpu.SemaphoreType.DMA,
            pltpu.SemaphoreType.DMA((SLOTS, groups)),
            pltpu.SemaphoreType.DMA((SLOTS, groups)),
            pltpu.SemaphoreType.DMA((REACH, groups)),
            pltpu.SemaphoreType.DMA((REACH, groups)),
            pltpu.SemaphoreType.DMA((groups,)),
        ],
        compiler_params=pltpu.CompilerParams(
            collective_id=0, has_side_effects=True, vmem_limit_bytes=56 * 1024 * 1024
        ),
        cost_estimate=pl.CostEstimate(
            flops=4 * tokens * (tokens + far) * width,
            bytes_accessed=4 * tokens * width * 2,
            transcendentals=heads * tokens * (tokens + far),
        ),
    )(queries, key_rows, values, block_lists, block_lists)


def solution(mesh):
    rows = P(("clip", "frame"), None)
    return jax.shard_map(
        functools.partial(local, mesh.shape["frame"]),
        mesh=mesh,
        in_specs=(rows, rows, rows, rows),
        out_specs=rows,
        check_vma=False,
    )
```

```python
import functools
import math

import jax
import jax.numpy as jnp
from jax import lax
from jax.experimental import pallas as pl
from jax.experimental.pallas import tpu as pltpu
from jax.sharding import PartitionSpec as P

HD = 128
REACH = 2
QUAD = 4
MOST_QUADS = 4
FIRST_GROUPS = 2
OWN_ROWS = 256
FAR_ROWS = 256
OFFSETS = (-1, 1, -2, 2)
SLOTS = len(OFFSETS)


def kernel(
    size,
    q_hbm,
    k_hbm,
    v_hbm,
    lists_smem,
    lists_vmem,
    out_hbm,
    q_ref,
    k_ref,
    v_ref,
    out_ref,
    named_vmem,
    named_smem,
    send_ref,
    recv_ref,
    acc_ref,
    peak_ref,
    total_ref,
    bias_ref,
    pick_ref,
    relay_ref,
    load_sem,
    list_send_sem,
    list_recv_sem,
    smem_sem,
    send_sem,
    recv_sem,
    relay_recv_sem,
    forward_sem,
    out_sem,
):
    me = lax.axis_index("frame")
    per_device, slots_row = lists_smem.shape
    tokens = q_ref.shape[0]
    block = tokens // per_device
    groups = recv_ref.shape[0]
    group_width = recv_ref.shape[3]
    scale = HD ** (-0.5) * math.log2(math.e)

    def inside(slot):
        other = me + OFFSETS[slot]
        return (other >= 0) & (other < size)

    parity = me % 2

    def near(slot):
        return parity == (1 if OFFSETS[slot] < 0 else 0)

    def place_of(slot):
        if slot >= 2:
            return slot * block
        return pl.multiple_of((1 - parity if slot == 0 else parity) * block, block)

    def place_there(slot):
        return place_of(slot) if slot < 2 else (slot ^ 1) * block

    loads = [
        pltpu.make_async_copy(k_hbm, k_ref, load_sem.at[0]),
        pltpu.make_async_copy(v_hbm, v_ref, load_sem.at[1]),
        pltpu.make_async_copy(q_hbm, q_ref, load_sem.at[2]),
    ]
    for load in loads:
        load.start()

    quads = size // QUAD
    quad = me // QUAD
    relays = size % QUAD == 0 and quads <= MOST_QUADS

    def by_relay(group, upward):
        share = jnp.where(upward, quads - 1 - quad, quad)
        return group * quads < groups * share

    def relayed(group, slot):
        other = me + OFFSETS[slot]
        return (other // QUAD != quad) & by_relay(group, OFFSETS[slot] > 0)

    lower = me % QUAD < QUAD // 2
    sign = jnp.where(lower, 1, -1)

    def forward_target(flow):
        return me + sign * (QUAD // 2 + 1 + flow)

    def forwards(group, flow):
        target = forward_target(flow)
        return (
            (target >= 0)
            & (target < size)
            & (target // QUAD == quad + sign)
            & by_relay(group, lower)
        )

    barrier = pltpu.get_barrier_semaphore()
    count = jnp.int32(0)
    span = REACH + QUAD // 2 if relays else REACH
    for offset in [o for o in range(-span, span + 1) if o]:
        present = (me + offset >= 0) & (me + offset < size)
        count = count + present.astype(jnp.int32)

        @pl.when(present)
        def _():
            pl.semaphore_signal(
                barrier,
                inc=1,
                device_id={"frame": me + offset},
                device_id_type=pl.DeviceIdType.MESH,
            )

    pl.semaphore_wait(barrier, count)

    def list_copy(slot):
        return pltpu.make_async_remote_copy(
            src_ref=lists_vmem,
            dst_ref=named_vmem.at[slot ^ 1],
            send_sem=list_send_sem.at[slot],
            recv_sem=list_recv_sem.at[slot ^ 1],
            device_id={"frame": me + OFFSETS[slot]},
            device_id_type=pl.DeviceIdType.MESH,
        )

    def list_arrival(slot):
        return pltpu.make_async_remote_copy(
            src_ref=lists_vmem,
            dst_ref=named_vmem.at[slot],
            send_sem=list_send_sem.at[slot],
            recv_sem=list_recv_sem.at[slot],
            device_id={"frame": me + OFFSETS[slot]},
            device_id_type=pl.DeviceIdType.MESH,
        )

    for slot in range(SLOTS):

        @pl.when(inside(slot))
        def _():
            list_copy(slot).start()

        @pl.when(jnp.logical_not(inside(slot)))
        def _():
            named_vmem[slot] = jnp.full((per_device, slots_row), -1, jnp.int32)
            for part in range(2):
                recv_ref[:, part, pl.ds(place_of(slot), block), :] = jnp.zeros(
                    (groups, block, group_width), jnp.bfloat16
                )

    for row in range(per_device):
        entries = [lists_smem[row, column] for column in range(slots_row)]
        for slot in range(SLOTS):
            first = (me + OFFSETS[slot]) * per_device
            named = jnp.bool_(False)
            for entry in entries:
                named = named | ((entry >= 0) & (entry >= first) & (entry < first + per_device))
            bias_ref[row * block : (row + 1) * block, pl.ds(place_of(slot), block)] = jnp.full(
                (block, block), jnp.where(named, 0.0, -jnp.inf), jnp.float32
            )

    for slot in range(SLOTS):

        @pl.when(inside(slot))
        def _():
            list_arrival(slot).wait_recv()

    to_smem = pltpu.make_async_copy(named_vmem, named_smem, smem_sem)
    to_smem.start()
    to_smem.wait()

    for slot in range(SLOTS):
        chosen = jnp.int32(0)
        for row in range(per_device):
            for column in range(slots_row):
                local_id = named_smem[slot, row, column] - me * per_device
                chosen = jnp.where((local_id >= 0) & (local_id < per_device), local_id, chosen)
        for place in range(per_device):
            pick_ref[slot, place] = jnp.full(
                (block, group_width), jnp.where(chosen == place, 1.0, 0.0), jnp.float32
            ).astype(jnp.bfloat16)

    loads[0].wait()
    loads[1].wait()

    def block_copy(group, slot):
        return pltpu.make_async_remote_copy(
            src_ref=send_ref.at[slot, group],
            dst_ref=recv_ref.at[group, :, pl.ds(place_there(slot), block), :],
            send_sem=send_sem.at[slot, group],
            recv_sem=recv_sem.at[slot ^ 1, group],
            device_id={"frame": me + OFFSETS[slot]},
            device_id_type=pl.DeviceIdType.MESH,
        )

    def block_arrival(group, slot):
        return pltpu.make_async_remote_copy(
            src_ref=send_ref.at[slot, group],
            dst_ref=recv_ref.at[group, :, pl.ds(place_of(slot), block), :],
            send_sem=send_sem.at[slot, group],
            recv_sem=recv_sem.at[slot, group],
            device_id={"frame": me + OFFSETS[slot]},
            device_id_type=pl.DeviceIdType.MESH,
        )

    def relay_copy(group, slot):
        step = QUAD // 2 if OFFSETS[slot] < 0 else -(QUAD // 2)
        flow = abs(OFFSETS[slot]) - 1
        return pltpu.make_async_remote_copy(
            src_ref=send_ref.at[slot, group],
            dst_ref=relay_ref.at[flow, group],
            send_sem=send_sem.at[slot, group],
            recv_sem=relay_recv_sem.at[flow, group],
            device_id={"frame": me + step},
            device_id_type=pl.DeviceIdType.MESH,
        )

    def relay_arrival(group, flow):
        return pltpu.make_async_remote_copy(
            src_ref=relay_ref.at[flow, group],
            dst_ref=relay_ref.at[flow, group],
            send_sem=forward_sem.at[flow, group],
            recv_sem=relay_recv_sem.at[flow, group],
            device_id={"frame": forward_target(flow)},
            device_id_type=pl.DeviceIdType.MESH,
        )

    def forward_copy(group, flow):
        slot = 2 * flow + jnp.where(lower, 0, 1)
        place = slot * block if flow else block
        return pltpu.make_async_remote_copy(
            src_ref=relay_ref.at[flow, group],
            dst_ref=recv_ref.at[group, :, pl.ds(pl.multiple_of(place, block), block), :],
            send_sem=forward_sem.at[flow, group],
            recv_sem=recv_sem.at[slot, group],
            device_id={"frame": forward_target(flow)},
            device_id_type=pl.DeviceIdType.MESH,
        )

    def forward_group(group):
        for flow in range(REACH):

            @pl.when(forwards(group, flow))
            def _():
                relay_arrival(group, flow).wait_recv()
                forward_copy(group, flow).start()

    def pick(group, slot):
        columns = pl.ds(pl.multiple_of(group * group_width, group_width), group_width)
        for part, source in enumerate((k_ref, v_ref)):
            picked = source[0:block, columns] * pick_ref[slot, 0]
            for choice in range(1, per_device):
                rows = slice(choice * block, (choice + 1) * block)
                picked = picked + source[rows, columns] * pick_ref[slot, choice]
            send_ref[slot, group, part] = picked

    def send_near(group, carry):
        for slot in (0, 1):

            @pl.when(near(slot) & inside(slot))
            def _():
                pick(group, slot)
                block_copy(group, slot).start()

        return carry

    def send_far(group, carry):
        for slot in (2, 3, 0, 1):
            leaves = inside(slot)
            if slot < 2:
                leaves = leaves & jnp.logical_not(near(slot))

            @pl.when(leaves)
            def _():
                pick(group, slot)
                if relays:
                    far_way = relayed(group, slot)

                    @pl.when(far_way)
                    def _():
                        relay_copy(group, slot).start()

                    @pl.when(jnp.logical_not(far_way))
                    def _():
                        block_copy(group, slot).start()

                else:
                    block_copy(group, slot).start()

        return carry

    lax.fori_loop(0, FIRST_GROUPS, send_far, 0)
    lax.fori_loop(0, groups, send_near, 0)
    lax.fori_loop(FIRST_GROUPS, groups, send_far, 0)

    loads[2].wait()

    def dot_t(left, right):
        return lax.dot_general(
            left, right, (((1,), (1,)), ((), ())), preferred_element_type=jnp.float32
        )

    def own_head(head, carry):
        columns = pl.ds(pl.multiple_of(head * HD, HD), HD)
        for slot in (0, 1):

            @pl.when(near(slot) & inside(slot))
            def _():
                block_arrival(head, slot).wait_recv()

        for start in range(0, tokens, OWN_ROWS):
            rows = slice(start, start + OWN_ROWS)
            queries = q_ref[rows, columns]
            scores = dot_t(queries, k_ref[:, columns])
            scores_near = dot_t(queries, recv_ref[head, 0, :block, :]) + bias_ref[rows, :block]
            peak = jnp.maximum(
                jnp.max(scores, axis=1, keepdims=True), jnp.max(scores_near, axis=1, keepdims=True)
            )
            weights = jnp.exp2((scores - peak) * scale)
            weights_near = jnp.exp2((scores_near - peak) * scale)
            peak_ref[head, rows] = peak
            total_ref[head, rows] = jnp.sum(weights, axis=1, keepdims=True) + jnp.sum(
                weights_near, axis=1, keepdims=True
            )
            acc_ref[rows, columns] = jnp.dot(
                weights.astype(jnp.bfloat16), v_ref[:, columns], preferred_element_type=jnp.float32
            ) + jnp.dot(
                weights_near.astype(jnp.bfloat16),
                recv_ref[head, 1, :block, :],
                preferred_element_type=jnp.float32,
            )
        return carry

    lax.fori_loop(0, groups, own_head, 0)

    def out_copy(group):
        columns = pl.ds(pl.multiple_of(group * group_width, group_width), group_width)
        return pltpu.make_async_copy(
            out_ref.at[:, columns], out_hbm.at[:, columns], out_sem.at[group]
        )

    def far_group(group, carry):
        if relays:
            forward_group(group)
        for slot in range(SLOTS):
            waits = inside(slot)
            if slot < 2:
                waits = waits & jnp.logical_not(near(slot))

            @pl.when(waits)
            def _():
                block_arrival(group, slot).wait_recv()

        columns = pl.ds(pl.multiple_of(group * HD, HD), HD)
        for start in range(0, tokens, FAR_ROWS):
            rows = slice(start, start + FAR_ROWS)
            scores = dot_t(q_ref[rows, columns], recv_ref[group, 0, block:, :])
            scores = scores + bias_ref[rows, block:]
            own_peak = peak_ref[group, rows]
            peak = jnp.maximum(jnp.max(scores, axis=1, keepdims=True), own_peak)
            weights = jnp.exp2((scores - peak) * scale)
            shrink = jnp.exp2((own_peak - peak) * scale)
            total = total_ref[group, rows] * shrink + jnp.sum(weights, axis=1, keepdims=True)
            far = jnp.dot(
                weights.astype(jnp.bfloat16),
                recv_ref[group, 1, block:, :],
                preferred_element_type=jnp.float32,
            )
            attended = (acc_ref[rows, columns] * shrink + far) / total
            out_ref[rows, columns] = attended.astype(jnp.bfloat16)
        out_copy(group).start()
        return carry

    lax.fori_loop(0, groups, far_group, 0)

    def finish(group, carry):
        for slot in range(SLOTS):

            @pl.when(inside(slot))
            def _():
                block_copy(group, slot).wait_send()

        if relays:
            for flow in range(REACH):

                @pl.when(forwards(group, flow))
                def _():
                    forward_copy(group, flow).wait_send()

        out_copy(group).wait()
        return carry

    lax.fori_loop(0, groups, finish, 0)
    for slot in range(SLOTS):

        @pl.when(inside(slot))
        def _():
            list_copy(slot).wait_send()


def local(size, queries, key_rows, values, block_lists):
    tokens, width = queries.shape
    per_device, slots_row = block_lists.shape
    block = tokens // per_device
    heads = width // HD
    groups = heads
    group_width = HD
    far = SLOTS * block
    hbm = pl.BlockSpec(memory_space=pl.ANY)
    return pl.pallas_call(
        functools.partial(kernel, size),
        out_shape=jax.ShapeDtypeStruct((tokens, width), jnp.bfloat16),
        in_specs=[
            hbm,
            hbm,
            hbm,
            pl.BlockSpec(memory_space=pltpu.SMEM),
            pl.BlockSpec(memory_space=pltpu.VMEM),
        ],
        out_specs=hbm,
        scratch_shapes=[
            pltpu.VMEM((tokens, width), jnp.bfloat16),
            pltpu.VMEM((tokens, width), jnp.bfloat16),
            pltpu.VMEM((tokens, width), jnp.bfloat16),
            pltpu.VMEM((tokens, width), jnp.bfloat16),
            pltpu.VMEM((SLOTS, per_device, slots_row), jnp.int32),
            pltpu.SMEM((SLOTS, per_device, slots_row), jnp.int32),
            pltpu.VMEM((SLOTS, groups, 2, block, group_width), jnp.bfloat16),
            pltpu.VMEM((groups, 2, far, group_width), jnp.bfloat16),
            pltpu.VMEM((tokens, width), jnp.float32),
            pltpu.VMEM((heads, tokens, 1), jnp.float32),
            pltpu.VMEM((heads, tokens, 1), jnp.float32),
            pltpu.VMEM((tokens, far), jnp.float32),
            pltpu.VMEM((SLOTS, per_device, block, group_width), jnp.bfloat16),
            pltpu.VMEM((REACH, groups, 2, block, group_width), jnp.bfloat16),
            pltpu.SemaphoreType.DMA((3,)),
            pltpu.SemaphoreType.DMA((SLOTS,)),
            pltpu.SemaphoreType.DMA((SLOTS,)),
            pltpu.SemaphoreType.DMA,
            pltpu.SemaphoreType.DMA((SLOTS, groups)),
            pltpu.SemaphoreType.DMA((SLOTS, groups)),
            pltpu.SemaphoreType.DMA((REACH, groups)),
            pltpu.SemaphoreType.DMA((REACH, groups)),
            pltpu.SemaphoreType.DMA((groups,)),
        ],
        compiler_params=pltpu.CompilerParams(
            collective_id=0, has_side_effects=True, vmem_limit_bytes=56 * 1024 * 1024
        ),
        cost_estimate=pl.CostEstimate(
            flops=4 * tokens * (tokens + far) * width,
            bytes_accessed=4 * tokens * width * 2,
            transcendentals=heads * tokens * (tokens + far),
        ),
    )(queries, key_rows, values, block_lists, block_lists)


def solution(mesh):
    rows = P(("clip", "frame"), None)
    return jax.shard_map(
        functools.partial(local, mesh.shape["frame"]),
        mesh=mesh,
        in_specs=(rows, rows, rows, rows),
        out_specs=rows,
        check_vma=False,
    )
```

```python
import functools
import math

import jax
import jax.numpy as jnp
from jax import lax
from jax.experimental import pallas as pl
from jax.experimental.pallas import tpu as pltpu
from jax.sharding import PartitionSpec as P

HD = 128
REACH = 2
QUAD = 4
MOST_QUADS = 4
FIRST_GROUPS = 2
OWN_ROWS = 256
FAR_ROWS = 256
OFFSETS = (-1, 1, -2, 2)
SLOTS = len(OFFSETS)


def kernel(
    size,
    q_hbm,
    k_hbm,
    v_hbm,
    lists_smem,
    lists_vmem,
    out_hbm,
    q_ref,
    k_ref,
    v_ref,
    out_ref,
    named_vmem,
    named_smem,
    send_ref,
    recv_ref,
    acc_ref,
    peak_ref,
    total_ref,
    bias_ref,
    pick_ref,
    relay_ref,
    load_sem,
    list_send_sem,
    list_recv_sem,
    smem_sem,
    send_sem,
    recv_sem,
    relay_recv_sem,
    forward_sem,
    out_sem,
):
    me = lax.axis_index("frame")
    per_device, slots_row = lists_smem.shape
    tokens = q_ref.shape[0]
    block = tokens // per_device
    groups = recv_ref.shape[0]
    group_width = recv_ref.shape[3]
    scale = HD ** (-0.5) * math.log2(math.e)

    def inside(slot):
        other = me + OFFSETS[slot]
        return (other >= 0) & (other < size)

    parity = me % 2

    def near(slot):
        return parity == (1 if OFFSETS[slot] < 0 else 0)

    def place_of(slot):
        if slot >= 2:
            return slot * block
        return pl.multiple_of((1 - parity if slot == 0 else parity) * block, block)

    def place_there(slot):
        return place_of(slot) if slot < 2 else (slot ^ 1) * block

    loads = [
        pltpu.make_async_copy(k_hbm, k_ref, load_sem.at[0]),
        pltpu.make_async_copy(v_hbm, v_ref, load_sem.at[1]),
        pltpu.make_async_copy(q_hbm, q_ref, load_sem.at[2]),
    ]
    loads[0].start()
    loads[1].start()

    quads = size // QUAD
    quad = me // QUAD
    relays = size % QUAD == 0 and quads <= MOST_QUADS

    def by_relay(group, upward):
        share = jnp.where(upward, quads - 1 - quad, quad)
        return group * quads < groups * share

    def relayed(group, slot):
        other = me + OFFSETS[slot]
        return (other // QUAD != quad) & by_relay(group, OFFSETS[slot] > 0)

    lower = me % QUAD < QUAD // 2
    sign = jnp.where(lower, 1, -1)

    def forward_target(flow):
        return me + sign * (QUAD // 2 + 1 + flow)

    def forwards(group, flow):
        target = forward_target(flow)
        return (
            (target >= 0)
            & (target < size)
            & (target // QUAD == quad + sign)
            & by_relay(group, lower)
        )

    barrier = pltpu.get_barrier_semaphore()
    count = jnp.int32(0)
    span = REACH + QUAD // 2 if relays else REACH
    for offset in [o for o in range(-span, span + 1) if o]:
        present = (me + offset >= 0) & (me + offset < size)
        count = count + present.astype(jnp.int32)

        @pl.when(present)
        def _():
            pl.semaphore_signal(
                barrier,
                inc=1,
                device_id={"frame": me + offset},
                device_id_type=pl.DeviceIdType.MESH,
            )

    pl.semaphore_wait(barrier, count)

    def list_copy(slot):
        return pltpu.make_async_remote_copy(
            src_ref=lists_vmem,
            dst_ref=named_vmem.at[slot ^ 1],
            send_sem=list_send_sem.at[slot],
            recv_sem=list_recv_sem.at[slot ^ 1],
            device_id={"frame": me + OFFSETS[slot]},
            device_id_type=pl.DeviceIdType.MESH,
        )

    def list_arrival(slot):
        return pltpu.make_async_remote_copy(
            src_ref=lists_vmem,
            dst_ref=named_vmem.at[slot],
            send_sem=list_send_sem.at[slot],
            recv_sem=list_recv_sem.at[slot],
            device_id={"frame": me + OFFSETS[slot]},
            device_id_type=pl.DeviceIdType.MESH,
        )

    for slot in range(SLOTS):

        @pl.when(inside(slot))
        def _():
            list_copy(slot).start()

        @pl.when(jnp.logical_not(inside(slot)))
        def _():
            named_vmem[slot] = jnp.full((per_device, slots_row), -1, jnp.int32)
            for part in range(2):
                recv_ref[:, part, pl.ds(place_of(slot), block), :] = jnp.zeros(
                    (groups, block, group_width), jnp.bfloat16
                )

    for row in range(per_device):
        entries = [lists_smem[row, column] for column in range(slots_row)]
        for slot in range(SLOTS):
            first = (me + OFFSETS[slot]) * per_device
            named = jnp.bool_(False)
            for entry in entries:
                named = named | ((entry >= 0) & (entry >= first) & (entry < first + per_device))
            bias_ref[row * block : (row + 1) * block, pl.ds(place_of(slot), block)] = jnp.full(
                (block, block), jnp.where(named, 0.0, -jnp.inf), jnp.float32
            )

    for slot in range(SLOTS):

        @pl.when(inside(slot))
        def _():
            list_arrival(slot).wait_recv()

    loads[2].start()
    to_smem = pltpu.make_async_copy(named_vmem, named_smem, smem_sem)
    to_smem.start()
    to_smem.wait()

    for slot in range(SLOTS):
        chosen = jnp.int32(0)
        for row in range(per_device):
            for column in range(slots_row):
                local_id = named_smem[slot, row, column] - me * per_device
                chosen = jnp.where((local_id >= 0) & (local_id < per_device), local_id, chosen)
        for place in range(per_device):
            pick_ref[slot, place] = jnp.full(
                (block, group_width), jnp.where(chosen == place, 1.0, 0.0), jnp.float32
            ).astype(jnp.bfloat16)

    loads[0].wait()
    loads[1].wait()

    def block_copy(group, slot):
        return pltpu.make_async_remote_copy(
            src_ref=send_ref.at[slot, group],
            dst_ref=recv_ref.at[group, :, pl.ds(place_there(slot), block), :],
            send_sem=send_sem.at[slot, group],
            recv_sem=recv_sem.at[slot ^ 1, group],
            device_id={"frame": me + OFFSETS[slot]},
            device_id_type=pl.DeviceIdType.MESH,
        )

    def block_arrival(group, slot):
        return pltpu.make_async_remote_copy(
            src_ref=send_ref.at[slot, group],
            dst_ref=recv_ref.at[group, :, pl.ds(place_of(slot), block), :],
            send_sem=send_sem.at[slot, group],
            recv_sem=recv_sem.at[slot, group],
            device_id={"frame": me + OFFSETS[slot]},
            device_id_type=pl.DeviceIdType.MESH,
        )

    def relay_copy(group, slot):
        step = QUAD // 2 if OFFSETS[slot] < 0 else -(QUAD // 2)
        flow = abs(OFFSETS[slot]) - 1
        return pltpu.make_async_remote_copy(
            src_ref=send_ref.at[slot, group],
            dst_ref=relay_ref.at[flow, group],
            send_sem=send_sem.at[slot, group],
            recv_sem=relay_recv_sem.at[flow, group],
            device_id={"frame": me + step},
            device_id_type=pl.DeviceIdType.MESH,
        )

    def relay_arrival(group, flow):
        return pltpu.make_async_remote_copy(
            src_ref=relay_ref.at[flow, group],
            dst_ref=relay_ref.at[flow, group],
            send_sem=forward_sem.at[flow, group],
            recv_sem=relay_recv_sem.at[flow, group],
            device_id={"frame": forward_target(flow)},
            device_id_type=pl.DeviceIdType.MESH,
        )

    def forward_copy(group, flow):
        slot = 2 * flow + jnp.where(lower, 0, 1)
        place = slot * block if flow else block
        return pltpu.make_async_remote_copy(
            src_ref=relay_ref.at[flow, group],
            dst_ref=recv_ref.at[group, :, pl.ds(pl.multiple_of(place, block), block), :],
            send_sem=forward_sem.at[flow, group],
            recv_sem=recv_sem.at[slot, group],
            device_id={"frame": forward_target(flow)},
            device_id_type=pl.DeviceIdType.MESH,
        )

    def forward_group(group):
        for flow in range(REACH):

            @pl.when(forwards(group, flow))
            def _():
                relay_arrival(group, flow).wait_recv()
                forward_copy(group, flow).start()

    def pick(group, slot):
        columns = pl.ds(pl.multiple_of(group * group_width, group_width), group_width)
        for part, source in enumerate((k_ref, v_ref)):
            picked = source[0:block, columns] * pick_ref[slot, 0]
            for choice in range(1, per_device):
                rows = slice(choice * block, (choice + 1) * block)
                picked = picked + source[rows, columns] * pick_ref[slot, choice]
            send_ref[slot, group, part] = picked

    def send_near(group, carry):
        for slot in (0, 1):

            @pl.when(near(slot) & inside(slot))
            def _():
                pick(group, slot)
                block_copy(group, slot).start()

        return carry

    def send_far(group, carry):
        for slot in (2, 3, 0, 1):
            leaves = inside(slot)
            if slot < 2:
                leaves = leaves & jnp.logical_not(near(slot))

            @pl.when(leaves)
            def _():
                pick(group, slot)
                if relays:
                    far_way = relayed(group, slot)

                    @pl.when(far_way)
                    def _():
                        relay_copy(group, slot).start()

                    @pl.when(jnp.logical_not(far_way))
                    def _():
                        block_copy(group, slot).start()

                else:
                    block_copy(group, slot).start()

        return carry

    lax.fori_loop(0, FIRST_GROUPS, send_far, 0)
    lax.fori_loop(0, groups, send_near, 0)
    lax.fori_loop(FIRST_GROUPS, groups, send_far, 0)

    loads[2].wait()

    def dot_t(left, right):
        return lax.dot_general(
            left, right, (((1,), (1,)), ((), ())), preferred_element_type=jnp.float32
        )

    def own_head(head, carry):
        columns = pl.ds(pl.multiple_of(head * HD, HD), HD)
        for slot in (0, 1):

            @pl.when(near(slot) & inside(slot))
            def _():
                block_arrival(head, slot).wait_recv()

        for start in range(0, tokens, OWN_ROWS):
            rows = slice(start, start + OWN_ROWS)
            queries = q_ref[rows, columns]
            scores = dot_t(queries, k_ref[:, columns])
            scores_near = dot_t(queries, recv_ref[head, 0, :block, :]) + bias_ref[rows, :block]
            peak = jnp.maximum(
                jnp.max(scores, axis=1, keepdims=True), jnp.max(scores_near, axis=1, keepdims=True)
            )
            weights = jnp.exp2((scores - peak) * scale)
            weights_near = jnp.exp2((scores_near - peak) * scale)
            peak_ref[head, rows] = peak
            total_ref[head, rows] = jnp.sum(weights, axis=1, keepdims=True) + jnp.sum(
                weights_near, axis=1, keepdims=True
            )
            acc_ref[rows, columns] = jnp.dot(
                weights.astype(jnp.bfloat16), v_ref[:, columns], preferred_element_type=jnp.float32
            ) + jnp.dot(
                weights_near.astype(jnp.bfloat16),
                recv_ref[head, 1, :block, :],
                preferred_element_type=jnp.float32,
            )
        return carry

    lax.fori_loop(0, groups, own_head, 0)

    def out_copy(group):
        columns = pl.ds(pl.multiple_of(group * group_width, group_width), group_width)
        return pltpu.make_async_copy(
            out_ref.at[:, columns], out_hbm.at[:, columns], out_sem.at[group]
        )

    def far_group(group, carry):
        if relays:

            @pl.when(group + 1 < groups)
            def _():
                forward_group(group + 1)

        for slot in range(SLOTS):
            waits = inside(slot)
            if slot < 2:
                waits = waits & jnp.logical_not(near(slot))

            @pl.when(waits)
            def _():
                block_arrival(group, slot).wait_recv()

        columns = pl.ds(pl.multiple_of(group * HD, HD), HD)
        for start in range(0, tokens, FAR_ROWS):
            rows = slice(start, start + FAR_ROWS)
            scores = dot_t(q_ref[rows, columns], recv_ref[group, 0, block:, :])
            scores = scores + bias_ref[rows, block:]
            own_peak = peak_ref[group, rows]
            peak = jnp.maximum(jnp.max(scores, axis=1, keepdims=True), own_peak)
            weights = jnp.exp2((scores - peak) * scale)
            shrink = jnp.exp2((own_peak - peak) * scale)
            total = total_ref[group, rows] * shrink + jnp.sum(weights, axis=1, keepdims=True)
            far = jnp.dot(
                weights.astype(jnp.bfloat16),
                recv_ref[group, 1, block:, :],
                preferred_element_type=jnp.float32,
            )
            attended = (acc_ref[rows, columns] * shrink + far) / total
            out_ref[rows, columns] = attended.astype(jnp.bfloat16)
        out_copy(group).start()
        return carry

    if relays:
        forward_group(0)
    lax.fori_loop(0, groups, far_group, 0)

    def finish(group, carry):
        for slot in range(SLOTS):

            @pl.when(inside(slot))
            def _():
                block_copy(group, slot).wait_send()

        if relays:
            for flow in range(REACH):

                @pl.when(forwards(group, flow))
                def _():
                    forward_copy(group, flow).wait_send()

        out_copy(group).wait()
        return carry

    lax.fori_loop(0, groups, finish, 0)
    for slot in range(SLOTS):

        @pl.when(inside(slot))
        def _():
            list_copy(slot).wait_send()


def local(size, queries, key_rows, values, block_lists):
    tokens, width = queries.shape
    per_device, slots_row = block_lists.shape
    block = tokens // per_device
    heads = width // HD
    groups = heads
    group_width = HD
    far = SLOTS * block
    hbm = pl.BlockSpec(memory_space=pl.ANY)
    return pl.pallas_call(
        functools.partial(kernel, size),
        out_shape=jax.ShapeDtypeStruct((tokens, width), jnp.bfloat16),
        in_specs=[
            hbm,
            hbm,
            hbm,
            pl.BlockSpec(memory_space=pltpu.SMEM),
            pl.BlockSpec(memory_space=pltpu.VMEM),
        ],
        out_specs=hbm,
        scratch_shapes=[
            pltpu.VMEM((tokens, width), jnp.bfloat16),
            pltpu.VMEM((tokens, width), jnp.bfloat16),
            pltpu.VMEM((tokens, width), jnp.bfloat16),
            pltpu.VMEM((tokens, width), jnp.bfloat16),
            pltpu.VMEM((SLOTS, per_device, slots_row), jnp.int32),
            pltpu.SMEM((SLOTS, per_device, slots_row), jnp.int32),
            pltpu.VMEM((SLOTS, groups, 2, block, group_width), jnp.bfloat16),
            pltpu.VMEM((groups, 2, far, group_width), jnp.bfloat16),
            pltpu.VMEM((tokens, width), jnp.float32),
            pltpu.VMEM((heads, tokens, 1), jnp.float32),
            pltpu.VMEM((heads, tokens, 1), jnp.float32),
            pltpu.VMEM((tokens, far), jnp.float32),
            pltpu.VMEM((SLOTS, per_device, block, group_width), jnp.bfloat16),
            pltpu.VMEM((REACH, groups, 2, block, group_width), jnp.bfloat16),
            pltpu.SemaphoreType.DMA((3,)),
            pltpu.SemaphoreType.DMA((SLOTS,)),
            pltpu.SemaphoreType.DMA((SLOTS,)),
            pltpu.SemaphoreType.DMA,
            pltpu.SemaphoreType.DMA((SLOTS, groups)),
            pltpu.SemaphoreType.DMA((SLOTS, groups)),
            pltpu.SemaphoreType.DMA((REACH, groups)),
            pltpu.SemaphoreType.DMA((REACH, groups)),
            pltpu.SemaphoreType.DMA((groups,)),
        ],
        compiler_params=pltpu.CompilerParams(
            collective_id=0, has_side_effects=True, vmem_limit_bytes=56 * 1024 * 1024
        ),
        cost_estimate=pl.CostEstimate(
            flops=4 * tokens * (tokens + far) * width,
            bytes_accessed=4 * tokens * width * 2,
            transcendentals=heads * tokens * (tokens + far),
        ),
    )(queries, key_rows, values, block_lists, block_lists)


def solution(mesh):
    rows = P(("clip", "frame"), None)
    return jax.shard_map(
        functools.partial(local, mesh.shape["frame"]),
        mesh=mesh,
        in_specs=(rows, rows, rows, rows),
        out_specs=rows,
        check_vma=False,
    )
```
